32 devices in a mesh: dp: 8 (over z, x), group: 4 (over y, core).
Axes of the slice: x: 2, y: 2, z: 4, core: 2. Of those that a mesh axis runs over, the one named last changes fastest.
Arguments:
- tokens_in: bfloat16 [16384, 768], P(('dp', 'group')), may hold values from -6 to 6
- cotangent: float32 [16384, 768], P(('dp', 'group')), may hold values from -6 to 6
- seq_lengths: int32 [32], P(('dp', 'group')), may hold values from 128 to 512, as said below
- drop_order: int32 [32, 512], P(('dp', 'group')), may hold values from 0 to 511, each once within a row
- routes: int32 [2, 16384, 2], P(None, ('dp', 'group')), may hold values from 0 to 7, all different within a row
- dense_master: float32 [4751360], P(('dp', 'group'))
- dense_moment: float32 [4751360], P(('dp', 'group')), may hold values from -0.00030517578 to 0.00030517578
- dense_second: float32 [4751360], P(('dp', 'group')), may hold values from 1e-09 to 1e-08
- expert_master: float32 [4, 2, 3, 2048, 768], P('group', None, None, 'dp')
- expert_moment: float32 [4, 2, 3, 2048, 768], P('group', None, None, 'dp'), may hold values from -0.00030517578 to 0.00030517578
- expert_second: float32 [4, 2, 3, 2048, 768], P('group', None, None, 'dp'), may hold values from 1e-09 to 1e-08
Outputs:
- output: bfloat16 [16384, 768], P(('dp', 'group'))
- grad_input: float32 [16384, 768], P(('dp', 'group'))
- dense_grad: float32 [4751360], P(('dp', 'group'))
- expert_grad: float32 [4, 2, 3, 2048, 768], P('group', None, None, 'dp')
- gain_grad: float32 [2, 2, 768], replicated
- dense_step: float32 [4751360], P(('dp', 'group'))
- expert_step: float32 [4, 2, 3, 2048, 768], P('group', None, None, 'dp')
The draws below stay inside these ranges and needn't reach their ends.
Inputs may be any that keep to these rules, and one draw needn't show every extreme that they name: `seq_lengths`: one device holds a sequence of 512 tokens. `drop_order`: each device's row is a permutation. `routes`: the two ids of a token differ; ids below 4 are feed-forward experts, 4 the zero expert, 5 the copy expert, the last two constant experts.
All inputs are finite; a program needn't handle non-finite values.
Results may differ from the reference program's by a relative error of at most 0.022.
Values may be sent and summed in bfloat16 or wider, within the bound.
No kernel may reach another device: no remote copies, remote signals or barrier semaphores. Data moves between devices by JAX's collectives and lax.ppermute only.
A program may use at most 256 MiB of HBM per device.

```python
import math
from functools import partial
import jax
import jax.numpy as jnp
from jax import lax

D = 768
HEADS = 12
HDIM = 64
FF = 2048
LAYERS = 2
TOK_DEV = 512
EXPERTS = 4
CAP = 90
DENSE = 4751360
TOKENS = 16384
DEVICES = 32


def noise_of(key, shape):
    return jax.random.normal(key, shape, jnp.float32)


def draw_seq_lengths(key, part):
    base = jax.random.randint(jax.random.fold_in(key, 11), (DEVICES,), TOK_DEV // 4, TOK_DEV + 1)
    where_long = jax.random.randint(jax.random.fold_in(key, 12), (), 0, DEVICES)
    return base.at[where_long].set(TOK_DEV).astype(jnp.int32)


def draw_dense_master(key, part):
    routed = EXPERTS + 4
    pieces = []
    index = 0
    used = 0
    for depth in range(LAYERS):
        specs = [(D * D, D ** (-0.5), 0.0), (D * D, D ** (-0.5), 0.0), (D * D, D ** (-0.5), 0.0), (D * D, 4.0 * D ** (-0.5), 0.0), (D * routed, 0.7 * D ** (-0.5), 0.0), (D * 4, D ** (-0.5), 0.0), (2 * D, 1.0, 0.0), (D, 0.15, 1.0), (D, 0.15, 1.0)]
        if depth > 0:
            specs.append((routed * routed, 0.5 * routed ** (-0.5), 0.0))
        for amount, scale, center in specs:
            pieces.append(center + scale * noise_of(jax.random.fold_in(key, 100 + index), (amount,)))
            index = index + 1
            used = used + amount
    pieces.append(0.02 * noise_of(jax.random.fold_in(key, 100 + index), (DENSE - used,)))
    return jnp.concatenate(pieces)


def draw_expert_master(key, part):
    scales = jnp.array([D ** (-0.5), D ** (-0.5), 2.5 * FF ** (-0.5)], jnp.float32)
    noise = noise_of(jax.random.fold_in(key, 21), (EXPERTS, LAYERS, 3, FF, D))
    return noise * scales[None, None, :, None, None]


def level_of(own_key, shape, shards, least, high):
    def one(axis_at, blocks):
        steps = jax.random.uniform(jax.random.fold_in(jax.random.fold_in(own_key, 6), axis_at), (blocks,), jnp.float32, least / len(shards), high / len(shards))
        return jnp.repeat(jnp.exp(steps), shape[axis_at] // blocks).reshape((-1,) + (1,) * (len(shape) - axis_at - 1))

    level = one(*shards[0])
    for cut in shards[1:]:
        level = level * one(*cut)
    return level


def distinct(key, rows, count, top, lift):
    sequence = jax.random.permutation(jax.random.fold_in(key, 1), count)
    favour = sequence
    for power in range(3):
        favour = favour * favour // count
    favour = favour * lift // count
    chance = jax.random.randint(jax.random.fold_in(key, 2), (rows, count), 0, 4096) + favour
    holders = jax.random.permutation(jax.random.fold_in(key, 3), rows)[jnp.arange(count) % rows]
    chance = jnp.where(jnp.arange(rows)[:, None] == holders[None, :], 1 << 14, chance)
    merit = chance * count + jnp.arange(count)
    return lax.top_k(merit.astype(jnp.int32), top)[1].astype(jnp.int32)


def scatter_about(own_key, shape, scale, most, cuts=(), kind=jnp.bfloat16):
    values = scale * jax.random.normal(own_key, shape, jnp.float32)
    if cuts:
        values = values * level_of(own_key, shape, cuts, -0.22, 0.18)
    return jnp.clip(values, -most, most).astype(kind)


def setup_inputs(seed: int = 0) -> dict:
    streams_of = jax.random.split(jax.random.key(seed), 12)
    return {
        "tokens_in": scatter_about(streams_of[0], (TOKENS, D), 1.0, 6.0, ((0, 32),)),
        "cotangent": scatter_about(streams_of[1], (TOKENS, D), 1.0, 6.0, ((0, 32),), jnp.float32),
        "seq_lengths": draw_seq_lengths(jax.random.fold_in(streams_of[11], 71), 0),
        "drop_order": jax.vmap(lambda own: jax.random.permutation(own, TOK_DEV))(jax.random.split(streams_of[3], DEVICES)).reshape((DEVICES, TOK_DEV)).astype(jnp.int32),
        "routes": distinct(streams_of[4], LAYERS * TOKENS, EXPERTS + 4, 2, 2048).reshape((LAYERS, TOKENS, 2)),
        "dense_master": draw_dense_master(jax.random.fold_in(streams_of[11], 71), 0),
        "dense_moment": scatter_about(streams_of[6], (DENSE,), 0.00002, 0.00030517578, ((0, 32),), jnp.float32),
        "dense_second": jnp.clip(jnp.exp(math.log(9.99999993922529e-09) - 2.3025851 * jax.random.uniform(streams_of[7], (DENSE,), jnp.float32) ** level_of(streams_of[7], (DENSE,), ((0, 32),), -0.2, 0.2)), 9.999999717180685e-10, 9.99999993922529e-09),
        "expert_master": draw_expert_master(jax.random.fold_in(streams_of[11], 71), 0),
        "expert_moment": scatter_about(streams_of[9], (EXPERTS, LAYERS, 3, FF, D), 0.00002, 0.00030517578, ((0, 4), (3, 8)), jnp.float32),
        "expert_second": jnp.clip(jnp.exp(math.log(9.99999993922529e-09) - 2.3025851 * jax.random.uniform(streams_of[10], (EXPERTS, LAYERS, 3, FF, D), jnp.float32) ** level_of(streams_of[10], (EXPERTS, LAYERS, 3, FF, D), ((0, 4), (3, 8)), -0.2, 0.2)), 9.999999717180685e-10, 9.99999993922529e-09),
    }


@jax.custom_vjp
def low(v):
    return lax.optimization_barrier(v.astype(jnp.bfloat16)).astype(jnp.float32)

@jax.custom_vjp
def low_back(v):
    return v

def low_keep(v):
    return (low(v), None)

def low_pass(kept, grad):
    return (grad,)

def back_keep(v):
    return (v, None)

def back_low(kept, grad):
    return (low(grad),)
low.defvjp(low_keep, low_pass)
low_back.defvjp(back_keep, back_low)
norm_eps = 1e-06
rope_base = 10000.0
neg_big = -1e+30
adam_rate = 0.001
beta_one = 0.9
beta_two = 0.95
adam_eps = 1e-08
decay_rate = 0.1
clip_norm = 1.0
step_number = 10

def matmul(form, left, right):
    return jnp.einsum(form, left, right, precision=lax.Precision.HIGHEST)

def layout(width, routed):
    items = []
    for depth in range(LAYERS):
        items = items + [(depth, 'query', (width, width)), (depth, 'key', (width, width)), (depth, 'value', (width, width)), (depth, 'output', (width, width)), (depth, 'router', (width, routed)), (depth, 'mixing', (width, 4)), (depth, 'constant', (2, width)), (depth, 'attn_gain', (width,)), (depth, 'moe_gain', (width,))]
        if depth > 0:
            items.append((depth, 'carry', (routed, routed)))
    return items

def unpack(flat, width, routed):
    params = [dict() for depth in range(LAYERS)]
    cursor = 0
    for depth, name, shape in layout(width, routed):
        amount = 1
        for extent in shape:
            amount = amount * extent
        params[depth][name] = flat[cursor:cursor + amount].reshape(shape)
        cursor = cursor + amount
    return params

def rms_norm(stream, gain):
    return stream * lax.rsqrt(lax.optimization_barrier(jnp.mean(stream * stream, axis=-1, keepdims=True)) + norm_eps) * gain

def rope_tables(count, half):
    position = jnp.arange(count, dtype=jnp.float32)[:, None]
    frequency = rope_base ** (-jnp.arange(half, dtype=jnp.float32) / half)
    angle = position * frequency[None, :]
    return (jnp.cos(angle)[:, None, :], jnp.sin(angle)[:, None, :])

def rotate(values, cosine, sine):
    half = values.shape[-1] // 2
    first, second = (values[..., :half], values[..., half:])
    return jnp.concatenate([first * cosine - second * sine, second * cosine + first * sine], axis=-1)

def visible(first, block, count, length):
    rows = first + jnp.arange(block)[:, None]
    cols = jnp.arange(count)[None, :]
    return (cols <= rows) & (cols < length)

def assign_slots(routes_now, order, length, experts, capacity):
    count = order.shape[0]
    live = jnp.arange(count) < length
    which = jnp.arange(experts)
    hits = (routes_now[:, :, None] == which[None, None, :]) & live[:, None, None]
    marks = lax.optimization_barrier(jnp.sum(hits.astype(jnp.int32), axis=1)).astype(jnp.int32)
    inverse = jnp.argsort(order).astype(jnp.int32)
    sorted_marks = marks[inverse]
    running = (jnp.cumsum(sorted_marks, axis=0) - sorted_marks).astype(jnp.int32)
    ranks = running[order.astype(jnp.int32)].astype(jnp.int32)
    rank_pick = lax.optimization_barrier(jnp.sum(jnp.where(hits, ranks[:, None, :], 0), axis=2)).astype(jnp.int32)
    kept = jnp.any(hits, axis=2) & (rank_pick < capacity)
    return jnp.where(kept, routes_now * capacity + rank_pick, experts * capacity).astype(jnp.int32)

def block_attention(rows, keys, values, length, first):
    count = keys.shape[0]
    block = rows.shape[0]
    scale = rows.shape[2] ** (-0.5)
    scores = low_back(matmul('qhd,khd->hqk', rows, keys) * scale)
    scores = jnp.where(visible(first, block, count, length)[None], scores, neg_big)
    probs = low(jax.nn.softmax(scores, axis=-1))
    return matmul('hqk,khd->qhd', probs, values)

def sequence_attention(packed):
    queries, keys, values, length = packed
    count = queries.shape[0]
    block = min(512, count)
    parts = []
    for first in range(0, count, block):
        parts.append(jax.checkpoint(partial(block_attention, first=first))(queries[first:first + block], keys, values, length))
    return jnp.concatenate(parts, axis=0)

def expert_block(packed):
    rows, weights = packed
    gate_value = low_back(matmul('rd,fd->rf', rows, weights[0]))
    up_value = low_back(matmul('rd,fd->rf', rows, weights[1]))
    hidden = low(jax.nn.silu(gate_value) * up_value)
    return low_back(low(matmul('rf,fd->rd', hidden, weights[2])))

def dispatch(normed_low, slot):
    empty = jnp.zeros((EXPERTS * CAP + 1, normed_low.shape[-1]), normed_low.dtype)
    return empty.at[slot.reshape(-1)].set(jnp.repeat(normed_low, 2, axis=0))[:-1]

def pick_rows(table, slot):
    return table[slot]

def adam_delta(master, moment, second, grad):
    moment_new = beta_one * moment + (1.0 - beta_one) * grad
    second_new = beta_two * second + (1.0 - beta_two) * grad * grad
    fix_one = 1.0 - beta_one ** step_number
    fix_two = 1.0 - beta_two ** step_number
    direction = moment_new / fix_one / (jnp.sqrt(second_new / fix_two) + adam_eps)
    return adam_rate * (direction + decay_rate * master)

def reference(tokens_in, cotangent, seq_lengths, drop_order, routes, dense_master, dense_moment, dense_second, expert_master, expert_moment, expert_second):
    routed = EXPERTS + 4
    dense_work = dense_master.astype(jnp.bfloat16).astype(jnp.float32)
    expert_work = expert_master.astype(jnp.bfloat16).astype(jnp.float32)
    stream_start = tokens_in.astype(jnp.float32).reshape(DEVICES, TOK_DEV, D)
    routes_dev = routes.reshape(LAYERS, DEVICES, TOK_DEV, 2)

    def slot_of(routes_now, order, length):
        return assign_slots(routes_now, order, length, EXPERTS, CAP)
    slots = [jax.vmap(slot_of)(routes_dev[depth], drop_order, seq_lengths) for depth in range(LAYERS)]
    cosine, sine = rope_tables(TOK_DEV, HDIM // 2)
    shape_heads = (DEVICES, TOK_DEV, HEADS, HDIM)

    def forward(stream, dense_flat, expert_all):
        params = unpack(dense_flat, D, routed)
        carry = None
        for depth in range(LAYERS):
            weights = params[depth]
            route_now = routes_dev[depth]
            slot = slots[depth]
            normed_low = low(rms_norm(stream, weights['attn_gain']))
            query = low_back(matmul('btd,de->bte', normed_low, weights['query']))
            keys = low_back(matmul('btd,de->bte', normed_low, weights['key']))
            values = low(low_back(matmul('btd,de->bte', normed_low, weights['value'])))
            query_rot = low(rotate(query.reshape(shape_heads), cosine, sine))
            keys_rot = low(rotate(keys.reshape(shape_heads), cosine, sine))
            mixed = lax.map(sequence_attention, (query_rot, keys_rot, values.reshape(shape_heads), seq_lengths))
            mixed = low_back(low(mixed.reshape(DEVICES, TOK_DEV, D)))
            middle = stream + low_back(matmul('btd,de->bte', mixed, weights['output']))
            normed_two = rms_norm(middle, weights['moe_gain'])
            normed_two_low = low(normed_two)
            logits = matmul('btd,de->bte', normed_two_low, weights['router'])
            if depth > 0:
                logits = logits + matmul('bte,ef->btf', carry, weights['carry'])
            chosen = jnp.take_along_axis(logits, route_now, axis=2)
            gates = jax.nn.softmax(chosen, axis=-1)
            sent = low_back(jax.vmap(dispatch)(normed_two_low, slot))
            by_expert = sent.reshape(DEVICES, EXPERTS, CAP, D).transpose(1, 0, 2, 3).reshape(EXPERTS, DEVICES * CAP, D)
            done = lax.map(jax.checkpoint(expert_block), (by_expert, expert_all[:, depth]))
            table = done.reshape(EXPERTS, DEVICES, CAP, D).transpose(1, 0, 2, 3).reshape(DEVICES, EXPERTS * CAP, D)
            table = jnp.concatenate([table, jnp.zeros((DEVICES, 1, D), jnp.float32)], axis=1)
            picked = jax.vmap(pick_rows)(table, slot)
            ffn_part = lax.optimization_barrier(jnp.sum(gates[..., None] * picked, axis=2))
            special = EXPERTS + jnp.arange(4)
            special_gates = lax.optimization_barrier(jnp.sum(gates[..., None] * (route_now[..., None] == special).astype(jnp.float32), axis=2))
            mix_logits = matmul('btd,dc->btc', normed_two, weights['mixing'])
            mix_first = jax.nn.softmax(mix_logits[..., 0:2], axis=-1)
            mix_second = jax.nn.softmax(mix_logits[..., 2:4], axis=-1)
            constant = weights['constant']
            constant_first = mix_first[..., 0:1] * normed_two + mix_first[..., 1:2] * constant[0]
            constant_second = mix_second[..., 0:1] * normed_two + mix_second[..., 1:2] * constant[1]
            routed_part = ffn_part + special_gates[..., 1:2] * normed_two + special_gates[..., 2:3] * constant_first + special_gates[..., 3:4] * constant_second
            stream = middle + routed_part
            carry = logits
        return stream
    result, pullback = jax.vjp(forward, stream_start, dense_work, expert_work)
    grad_stream, grad_dense, grad_expert = pullback(cotangent.reshape(DEVICES, TOK_DEV, D))
    square_sum = jnp.sum(grad_dense * grad_dense) + jnp.sum(grad_expert * grad_expert)
    factor = jnp.minimum(1.0, clip_norm / (jnp.sqrt(square_sum) + 1e-06))
    dense_clip = grad_dense * factor
    expert_clip = grad_expert * factor
    grad_params = unpack(grad_dense, D, routed)
    gain_grad = jnp.stack([jnp.stack([grad_params[depth]['attn_gain'], grad_params[depth]['moe_gain']], axis=0) for depth in range(LAYERS)], axis=0) * factor
    dense_step = adam_delta(dense_master, dense_moment, dense_second, dense_clip)
    expert_step = adam_delta(expert_master, expert_moment, expert_second, expert_clip)
    return (result.reshape(TOKENS, D).astype(jnp.bfloat16), grad_stream.reshape(TOKENS, D), dense_clip, expert_clip, gain_grad, dense_step, expert_step)
```

```python
import functools

import jax
import numpy as np
import jax.numpy as jnp
from jax import lax
from jax.experimental import pallas as pl
from jax.experimental.pallas import tpu as pltpu
from jax.sharding import PartitionSpec as P

HEADS = 12
LAYERS = 2


norm_eps = 1e-06
rope_base = 10000.0
neg_big = -1e30
adam_rate = 0.001
beta_one = 0.9
beta_two = 0.95
adam_eps = 1e-08
decay_rate = 0.1
clip_norm = 1.0
step_number = 10
highest = lax.Precision.HIGHEST
f32 = jnp.float32
bf16 = jnp.bfloat16
ALL = ("dp", "group")


def layout(width, routed):
    items = []
    for depth in range(LAYERS):
        items = items + [
            (depth, "query", (width, width)),
            (depth, "key", (width, width)),
            (depth, "value", (width, width)),
            (depth, "output", (width, width)),
            (depth, "router", (width, routed)),
            (depth, "mixing", (width, 4)),
            (depth, "constant", (2, width)),
            (depth, "attn_gain", (width,)),
            (depth, "moe_gain", (width,)),
        ]
        if depth > 0:
            items.append((depth, "carry", (routed, routed)))
    return items


def unpack(flat, width, routed):
    params = [dict() for depth in range(LAYERS)]
    cursor = 0
    for depth, name, shape in layout(width, routed):
        amount = 1
        for extent in shape:
            amount = amount * extent
        params[depth][name] = flat[cursor : cursor + amount].reshape(shape)
        cursor = cursor + amount
    return params


class Wires:
    def __init__(self):
        self.groups = lax.axis_size("group")
        self.dp = lax.axis_size("dp")
        self.tops = self.dp // 4
        self.me_dp = lax.axis_index("dp")
        self.me_group = lax.axis_index("group")

    def swap(self, array, h=0, l=0, x=0, g=0):
        off = h * 4 + l * 2 + x
        pairs = [
            (d * self.groups + k, (d ^ off) * self.groups + (k ^ g))
            for d in range(self.dp)
            for k in range(self.groups)
        ]
        return lax.ppermute(array, ALL, pairs)


def pin(values, *after):
    return lax.optimization_barrier((values, after))[0]


def axis_step(axis):
    return dict(l=dict(l=1), x=dict(x=1), y=dict(g=2), c=dict(g=1))[axis]


AXIS_VALUE = dict(l=8, x=4, y=2, c=1)


def plan_thirds(tiles):
    step = tiles // 3
    first = tiles - 2 * step
    return (
        (("l", "x", "y"), 0, first),
        (("x", "y", "l"), first, step),
        (("y", "l", "x"), first + step, step),
    )


def plan_halves(tiles):
    half = tiles // 2
    return ((("l", "x", "y"), 0, tiles - half), (("l", "y", "x"), tiles - half, half))


def grow(wires, parts, plan, step):
    return [
        jnp.concatenate([v, wires.swap(v, **axis_step(axes[step]))], axis=0)
        for v, (axes, _, _) in zip(parts, plan)
    ]


class ScatterDense:
    def __init__(self, wires, halves, plan):
        self.wires = wires
        self.halves = halves
        self.plan = plan

    def send(self, step, *after):
        self.got = []
        for (_, give), (axes, _, _) in zip(self.halves, self.plan):
            axis = (("c",) + axes[::-1])[step]
            give = pin(give, *after) if after else give
            self.got.append(self.wires.swap(give, **axis_step(axis)))

    def add(self):
        halves = []
        for (keep, _), got in zip(self.halves, self.got):
            if keep.shape[0] == 1:
                halves.append(((keep[0].astype(f32) + got[0].astype(f32)).astype(bf16), None))
                continue
            half = keep.shape[0] // 2
            cut = lambda a, b: (keep[a:b].astype(f32) + got[a:b].astype(f32)).astype(bf16)
            halves.append((cut(0, half), cut(half, 2 * half)))
        self.halves = halves

    def done(self):
        return jnp.concatenate([keep for keep, _ in self.halves], axis=0)


def cut_far(part):
    half = part.shape[1] // 2
    return [part[:, :half], part[:, half:]]


class ScatterExpert:
    def __init__(self, wires, parts):
        self.wires = wires
        self.near = parts[:2]
        self.far = parts[2:]

    def first(self):
        self.got = [self.wires.swap(v, x=1) for v in self.far[1::2]]

    def second(self, *after):
        sums = [
            (pin(a, *after).astype(f32) + b.astype(f32)).astype(bf16)
            for a, b in zip(self.far[0::2], self.got)
        ]
        self.got_far = [self.wires.swap(v, h=1 + i // 2) for i, v in enumerate(sums)]
        self.got_near = self.wires.swap(pin(self.near[1], *sums), x=1)

    def received(self):
        return [*self.got_far, self.got_near]

    def done(self):
        total = self.near[0].astype(f32) + self.got_near.astype(f32)
        for i in range(0, len(self.got_far), 2):
            total = total + jnp.concatenate(self.got_far[i : i + 2], axis=1).astype(f32)
        return total


def exchange_out(wires, pairs, after=()):
    half = len(pairs)
    got = [pairs[0]]
    for l in range(2):
        for y in range(half):
            if l or y:
                got.append(wires.swap(pairs[y], l=l, g=2 * y))
    room = pairs[0].shape[0] // 2
    crossed = wires.swap(jnp.concatenate([v[room:] for v in got], axis=0), g=1)
    return [*got, crossed]


def exchange_back(wires, near, crossed):
    count = 2 * (wires.groups // 2)
    room = near.shape[0] // count
    other = wires.swap(crossed, g=1)
    got = []
    for i in range(count):
        l, y = divmod(i, wires.groups // 2)
        s = slice(i * room, (i + 1) * room)
        pair = jnp.concatenate([near[s], other[s]], axis=0)
        got.append(pair if i == 0 else wires.swap(pair, l=l, g=2 * y))
    return got


def adam_delta(master, moment, second, grad):
    moment_new = beta_one * moment + (1.0 - beta_one) * grad
    second_new = beta_two * second + (1.0 - beta_two) * grad * grad
    fix_one = 1.0 - beta_one**step_number
    fix_two = 1.0 - beta_two**step_number
    direction = moment_new / fix_one / (jnp.sqrt(second_new / fix_two) + adam_eps)
    return adam_rate * (direction + decay_rate * master)


VM = pl.BlockSpec(memory_space=pltpu.VMEM)
SM = pl.BlockSpec(memory_space=pltpu.SMEM)
ANY = pl.BlockSpec(memory_space=pl.ANY)
LANES = 128
MIX = 32
SLOT = 48
INV = 50
PARAMS = dict(vmem_limit_bytes=60 * 1024 * 1024)


def dot(a, b):
    return lax.dot_general(a, b, (((1,), (0,)), ((), ())), preferred_element_type=f32)


def dot_nt(a, b):
    return lax.dot_general(a, b, (((1,), (1,)), ((), ())), preferred_element_type=f32)


def dot_tn(a, b):
    return lax.dot_general(a, b, (((0,), (0,)), ((), ())), preferred_element_type=f32)


def split(v):
    high = v.astype(bf16)
    return high, (v - high.astype(f32)).astype(bf16)


def lane_of(rows):
    return lax.broadcasted_iota(jnp.int32, (rows, LANES), 1)


def take_lane(v, lane, at):
    return jnp.sum(jnp.where(lane == at, v, 0.0), axis=1, keepdims=True)


def put_lanes(lane, pairs):
    out = jnp.zeros(lane.shape, f32)
    for at, column in pairs:
        out = jnp.where(lane == at, column, out)
    return out


def blocks(count, size, body):
    def step(i, none):
        body(pl.multiple_of(i * size, size))
        return none

    lax.fori_loop(0, count // size, step, 0)


def half_mask(hd):
    lane = lane_of(1)
    mine = lane < 64 if hd == 0 else lane >= 64
    return jnp.where(mine, 1.0, 0.0).astype(bf16)


def rope_turn(v, cos, sin, lane):
    other = jnp.where(lane % 64 < 32, pltpu.roll(v, 96, 1), pltpu.roll(v, 32, 1))
    return v * cos + other * sin


def two_softmax(a, b):
    top = jnp.maximum(a, b)
    ea, eb = jnp.exp(a - top), jnp.exp(b - top)
    total = ea + eb
    return ea / total, eb / total


class Columns:
    def __init__(self, side, routes, groups):
        lane = lane_of(side.shape[0])
        self.lane = lane
        self.routes = [routes[:, k : k + 1] for k in range(2)]
        self.hot = [lane == r for r in self.routes]
        chosen = [jnp.sum(jnp.where(h, side, 0.0), axis=1, keepdims=True) for h in self.hot]
        self.gates = two_softmax(*chosen)
        mixes = [take_lane(side, lane, MIX + j) for j in range(4)]
        self.first = two_softmax(mixes[0], mixes[1])
        self.second = two_softmax(mixes[2], mixes[3])
        self.special = [
            sum(jnp.where(self.routes[k] == groups + j, self.gates[k], 0.0) for k in range(2))
            for j in range(4)
        ]
        self.normed_part = (
            self.special[1]
            + self.special[2] * self.first[0]
            + self.special[3] * self.second[0]
        )
        self.constant_part = (self.special[2] * self.first[1], self.special[3] * self.second[1])
        self.slots = [take_lane(side, lane, SLOT + k) for k in range(2)]
        self.inverse = take_lane(side, lane, INV)
        self.inverse_two = take_lane(side, lane, INV + 1)


def add_tables(back, table, room):
    half = len(back) // 2
    for y in range(half):

        def add(r, y=y):
            s = pl.ds(r, 16)
            total = back[y][s, :].astype(f32) + back[half + y][s, :].astype(f32)
            table[pl.ds(2 * y * room + r, 16), :] = total.astype(bf16)

        blocks(2 * room, 16, add)


def combine_body(cols, mid, ret, vecs, table, hots, out, room):
    count, width = mid.shape
    rows = table.shape[0]
    add_tables(ret, table, room)
    at = lax.broadcasted_iota(jnp.int32, (count, rows), 1).astype(f32)
    for k in range(2):
        hots[k][...] = jnp.where(at == cols.slots[k], 1.0, 0.0).astype(bf16)

    def piece(c):
        s = pl.ds(c, LANES)
        m = mid[:, s]
        normed = m * cols.inverse_two * vecs[3:4, s]
        y = m + cols.gates[0] * dot(hots[0][...], table[:, s])
        y = y + cols.gates[1] * dot(hots[1][...], table[:, s])
        y = y + cols.normed_part * normed
        y = y + cols.constant_part[0] * vecs[0:1, s] + cols.constant_part[1] * vecs[1:2, s]
        out[:, s] = y.astype(out.dtype)

    blocks(width, LANES, piece)


def visible_bias(bias, length, flip):
    count = bias.shape[0]

    def piece(r):
        shape = (32, count)
        a = lax.broadcasted_iota(jnp.int32, shape, 0) + r
        b = lax.broadcasted_iota(jnp.int32, shape, 1)
        key, query = (a, b) if flip else (b, a)
        bias[pl.ds(r, 32), :] = jnp.where((key <= query) & (key < length), 0.0, neg_big)

    blocks(count, 32, piece)


def forward_kernel(static, *refs):
    depth, groups, capacity, room, eps, n_after = static
    refs = list(refs)
    take = lambda n: [refs.pop(0) for _ in range(n)]
    ints, order_row, order_col, routes, w_hbm, wsm, vecs, cos, sin = take(9)
    if depth == 0:
        (source,) = take(1)
    else:
        side_in, routes_in, mid_in, vecs_in, wg, cot = take(6)
        ret = take(groups)
    take(n_after)
    send = take(groups // 2)
    if depth > 0:
        send_grads = take(groups // 2)
    n1, q_out, k_out, v_out, mixed, lse_out, middle, side_out = take(8)
    if depth > 0:
        (stream,) = take(1)
    w, bias, n2h, n2l, lse, sems = take(6)
    if depth > 0:
        table, hot0, hot1 = take(3)
    count, width = n1.shape
    routed = groups + 4
    length, me = ints[0], ints[1]
    loads = [pltpu.make_async_copy(w_hbm.at[i], w.at[i], sems.at[i]) for i in range(4)]
    for c in loads:
        c.start()
    visible_bias(bias, length, False)
    lane = lane_of(count)

    if depth > 0:
        before = Columns(side_in[...], routes_in[...], groups)
        combine_body(before, mid_in, ret, vecs_in, table, (hot0, hot1), stream, room)
        source = stream

    def norm_one(r):
        s = pl.ds(r, 64)
        x = source[s, :].astype(f32)
        inverse = lax.rsqrt(jnp.mean(x * x, axis=1, keepdims=True) + eps)
        n1[s, :] = (x * inverse * vecs[2:3, :]).astype(bf16)
        side_out[s, :] = jnp.where(lane_of(64) == INV, inverse, 0.0)

    blocks(count, 64, norm_one)

    for kind in range(3):
        loads[kind].wait()

        def project(c, kind=kind):
            s = pl.ds(c, 256)
            y = dot(n1[...], w[kind, :, s])
            for half in range(2):
                part = y[:, half * LANES : (half + 1) * LANES]
                t = pl.ds(pl.multiple_of(c + half * LANES, LANES), LANES)
                if kind == 2:
                    v_out[:, t] = part.astype(bf16)
                else:
                    part = rope_turn(part, cos[...], sin[...], lane)
                    if kind == 0:
                        q_out[:, t] = (part * 0.125).astype(bf16)
                    else:
                        k_out[:, t] = part.astype(bf16)

        blocks(width, 256, project)

    half_rows = count // 2

    def attend_pair(c):
        t = pl.ds(c, LANES)
        pair = c // LANES
        for qb in range(2):
            rows = pl.ds(qb * half_rows, half_rows)
            span = (qb + 1) * half_rows
            q2 = q_out[rows, t]
            k2 = k_out[0:span, t]
            v2 = v_out[0:span, t]
            low_half = lane_of(half_rows) < 64
            outs = []
            for hd in range(2):
                qm = q2 * half_mask(hd)
                s = dot_nt(qm, k2) + bias[rows, 0:span]
                peak = jnp.max(s, axis=1, keepdims=True)
                e = jnp.exp(s - peak)
                total = jnp.sum(e, axis=1, keepdims=True)
                outs.append(dot(e.astype(bf16), v2) * (1.0 / total))
                lse[rows, :] = jnp.where(
                    lane_of(half_rows) == 2 * pair + hd, peak + jnp.log(total), lse[rows, :]
                )
            mixed[rows, t] = jnp.where(low_half, outs[0], outs[1]).astype(bf16)

    lse[...] = jnp.zeros(lse.shape, f32)
    blocks(width, LANES, attend_pair)
    lse_out[...] = jnp.transpose(lse[...])[0:16, :]
    loads[3].wait()

    def mix_out(c):
        s = pl.ds(c, 256)
        middle[:, s] = source[:, s].astype(f32) + dot(mixed[...], w[3, :, s])

    blocks(width, 256, mix_out)

    def norm_two(r):
        s = pl.ds(r, 64)
        x = middle[s, :]
        inverse = lax.rsqrt(jnp.mean(x * x, axis=1, keepdims=True) + eps)
        high, rest = split(x * inverse * vecs[3:4, :])
        n2h[s, :] = high
        n2l[s, :] = rest
        side_out[s, :] = side_out[s, :] + jnp.where(lane_of(64) == INV + 1, inverse, 0.0)

    blocks(count, 64, norm_two)
    both = dot(n2h[...], wsm[...])
    rest = dot(n2l[...], wsm[...])
    logits = jnp.where(lane < routed, both, 0.0)
    if depth > 0:
        held = jnp.where(lane < routed, side_in[...], 0.0)
        h1, h2 = split(held)
        h3 = (held - h1.astype(f32) - h2.astype(f32)).astype(bf16)
        logits = logits + dot(h1, wg[...]) + dot(h2, wg[...]) + dot(h3, wg[...])
    mixes = jnp.where((lane >= MIX) & (lane < MIX + 4), both + rest, 0.0)
    r = [routes[:, k : k + 1] for k in range(2)]
    token = lax.broadcasted_iota(jnp.int32, (count, 1), 0)
    live = token < length
    other = lax.broadcasted_iota(jnp.int32, (count, count), 1)
    earlier = jnp.where((order_row[...] < order_col[...]) & (other < length), 1.0, 0.0).astype(bf16)
    marks = jnp.where((lane == r[0]) | (lane == r[1]), 1.0, 0.0).astype(bf16)
    ranks = dot(earlier, marks)
    slots = []
    for k in range(2):
        rank = take_lane(ranks, lane, r[k])
        kept = (r[k] < groups) & live & (rank < capacity)
        slots.append(jnp.where(kept, ((r[k] ^ me) * room).astype(f32) + rank, -1.0))
    side = side_out[...] + logits + mixes
    side = side + jnp.where(lane == SLOT, slots[0], 0.0) + jnp.where(lane == SLOT + 1, slots[1], 0.0)
    side_out[...] = side
    turned = jnp.transpose(side)
    rows = groups * room
    at = lax.broadcasted_iota(jnp.int32, (rows, count), 0).astype(f32)
    is0 = at == turned[SLOT : SLOT + 1, :]
    is1 = at == turned[SLOT + 1 : SLOT + 2, :]
    place = jnp.where(is0 | is1, 1.0, 0.0).astype(bf16)

    def put(c):
        s = pl.ds(c, 256)
        put_blocks(send, dot(place, n2h[:, s]).astype(bf16), s, room)

    blocks(width, 256, put)
    if depth > 0:
        now = Columns(side, routes[...], groups)
        put_grads(now.gates, is0, is1, cot, send_grads, room)


def put_blocks(send, y, s, room):
    for i in range(len(send)):
        send[i][:, s] = y[2 * i * room : 2 * (i + 1) * room]


def put_grads(gates, is0, is1, grads, send, room):
    p0 = jnp.where(is0, 1.0, 0.0).astype(bf16)
    p1 = jnp.where(is1, 1.0, 0.0).astype(bf16)

    def put(c):
        s = pl.ds(c, LANES)
        g = grads[:, s]
        y = dot(p0, (gates[0] * g).astype(bf16)) + dot(p1, (gates[1] * g).astype(bf16))
        put_blocks(send, y.astype(bf16), s, room)

    blocks(grads.shape[1], LANES, put)


def layer_forward(depth, sizes, ints, order, routes, weights, source, tables, after=()):
    groups, capacity, room = sizes
    count, width = routes.shape[0], weights["w"].shape[1]
    sds = jax.ShapeDtypeStruct
    low = sds((count, width), bf16)
    pair = sds((2 * room, width), bf16)
    outs = [pair] * (groups // 2 * (depth + 1)) + [
        low,
        low,
        low,
        low,
        low,
        sds((16, count), f32),
        sds((count, width), f32),
        sds((count, LANES), f32),
    ]
    scratch = [
        pltpu.VMEM((4, width, width), bf16),
        pltpu.VMEM((count, count), f32),
        pltpu.VMEM((count, width), bf16),
        pltpu.VMEM((count, width), bf16),
        pltpu.VMEM((count, LANES), f32),
        pltpu.SemaphoreType.DMA((4,)),
    ]
    args = [
        ints,
        order.reshape(1, count),
        order.reshape(count, 1),
        routes,
        weights["w"],
        weights["small"],
        weights["vecs"],
        *tables,
    ]
    specs = [SM, VM, VM, VM, ANY, VM, VM, VM, VM]
    if depth > 0:
        outs += [sds((count, width), f32)]
        scratch += [
            pltpu.VMEM((groups * room, width), bf16),
            pltpu.VMEM((count, groups * room), bf16),
            pltpu.VMEM((count, groups * room), bf16),
        ]
    args += list(source) + list(after)
    specs += [VM] * len(source) + [ANY] * len(after)
    got = pl.pallas_call(
        functools.partial(forward_kernel, (depth, groups, capacity, room, norm_eps, len(after))),
        out_shape=outs,
        in_specs=specs,
        out_specs=[VM] * len(outs),
        scratch_shapes=scratch,
        compiler_params=pltpu.CompilerParams(**PARAMS),
        cost_estimate=pl.CostEstimate(
            flops=6 * 10**9, bytes_accessed=20 * 10**6, transcendentals=4 * 10**6
        ),
        name="layer_forward",
    )(*args)
    return list(got)


def expert_kernel(static, *refs):
    sizes, pairs, room, back, n_after = static
    refs = list(refs)
    take = lambda n: [refs.pop(0) for _ in range(n)]
    n = len(sizes)
    parts = take(n)
    row_blocks = take(pairs + 1)
    if back:
        grad_blocks = take(pairs + 1)
    take(n_after)
    near, crossed = take(2)
    if back:
        grad_parts = take(n)
    w, sems, row_sems, rows = take(4)
    if back:
        (grads,) = take(1)
    (acc,) = take(1)

    def bring(source, to, sem):
        out = [
            pltpu.make_async_copy(source[i].at[0:room], to.at[i * room : (i + 1) * room], sem.at[i])
            for i in range(pairs)
        ]
        rest = pl.ds(pairs * room, pairs * room)
        return out + [pltpu.make_async_copy(source[pairs], to.at[rest], sem.at[pairs])]

    first = bring(row_blocks, rows, row_sems.at[0])
    if back:
        first += bring(grad_blocks, grads, row_sems.at[1])
    starts = [sum(sizes[:i]) for i in range(n)]
    loads = [
        pltpu.make_async_copy(parts[i], w.at[:, pl.ds(starts[i], sizes[i]), :], sems.at[i])
        for i in range(n)
    ]
    for c in first + loads:
        c.start()
    for c in first:
        c.wait()
    turns = []
    for i in range(n):
        if not turns or sum(sizes[j] for j in turns[-1]) >= 256:
            turns.append([])
        turns[-1].append(i)
    for turn, members in enumerate(turns):
        for i in members:
            loads[i].wait()
        here = pl.ds(starts[members[0]], sum(sizes[i] for i in members))
        gate = dot_nt(rows[...], w[0, here, :])
        up = dot_nt(rows[...], w[1, here, :])
        sigmoid = 1.0 / (1.0 + jnp.exp(-gate))
        act = gate * sigmoid
        hidden = (act * up).astype(bf16)
        if back:
            grad_hidden = dot_nt(grads[...], w[2, here, :])
            grad_up = (grad_hidden * act).astype(bf16)
            grad_gate = (
                grad_hidden * up * (sigmoid * (1.0 + gate * (1.0 - sigmoid)))
            ).astype(bf16)
            y = dot(grad_gate, w[0, here, :]) + dot(grad_up, w[1, here, :])
            kinds = (
                dot_tn(grad_gate, rows[...]).astype(bf16),
                dot_tn(grad_up, rows[...]).astype(bf16),
                dot_tn(hidden, grads[...]).astype(bf16),
            )
            for kind in range(3):
                for i in members:
                    begin = starts[i] - starts[members[0]]
                    grad_parts[i][kind] = kinds[kind][begin : begin + sizes[i], :]
        else:
            y = dot(hidden, w[2, here, :])
        if turn > 0:
            y = acc[...] + y
        if turn < len(turns) - 1:
            acc[...] = y
        else:
            near[...] = y[: pairs * room].astype(bf16)
            crossed[...] = y[pairs * room :].astype(bf16)


def run_expert(parts, row_blocks, grad_blocks, room, after=()):
    width = row_blocks[0].shape[1]
    sizes = tuple(p.shape[1] for p in parts)
    n, pairs = len(parts), len(row_blocks) - 1
    count = 2 * pairs * room
    sds = jax.ShapeDtypeStruct
    back = grad_blocks is not None
    args = [*parts, *row_blocks, *(grad_blocks or []), *after]
    outs = [sds((pairs * room, width), bf16)] * 2
    outs += [sds(p.shape, bf16) for p in parts] if back else []
    low = pltpu.VMEM((count, width), bf16)
    scratch = [
        pltpu.VMEM((3, sum(sizes), width), bf16),
        pltpu.SemaphoreType.DMA((n,)),
        pltpu.SemaphoreType.DMA((2, pairs + 1)),
    ]
    scratch += [low] * (1 + int(back)) + [pltpu.VMEM((count, width), f32)]
    work = 6 * count * sum(sizes) * width * (3 if back else 1)
    got = pl.pallas_call(
        functools.partial(expert_kernel, (sizes, pairs, room, back, len(after))),
        out_shape=outs,
        in_specs=[ANY] * len(args),
        out_specs=[VM] * len(outs),
        scratch_shapes=scratch,
        compiler_params=pltpu.CompilerParams(**PARAMS),
        cost_estimate=pl.CostEstimate(
            flops=work, bytes_accessed=12 * 10**6, transcendentals=count * sum(sizes)
        ),
        name="expert",
    )(*args)
    return got[0], got[1], list(got[2:])


def fold_matrix(routed, width):
    a = lax.broadcasted_iota(jnp.int32, (LANES, LANES), 0)
    b = lax.broadcasted_iota(jnp.int32, (LANES, LANES), 1)
    return jnp.where((a % width) + routed == b, 1.0, 0.0).astype(bf16)


def row_picks(count, per):
    a = lax.broadcasted_iota(jnp.int32, (count, count // per), 0)
    b = lax.broadcasted_iota(jnp.int32, (count, count // per), 1)
    return jnp.where(a // per == b, 1.0, 0.0).astype(bf16)


def own_lanes(count, width):
    a = lax.broadcasted_iota(jnp.int32, (count, LANES), 0)
    b = lax.broadcasted_iota(jnp.int32, (count, LANES), 1)
    return (a % (LANES // width)) == (b // width)


def unpack_kernel(static, *refs):
    depth, routed, width, tiles, plan, n_after = static
    refs = list(refs)
    take = lambda n: [refs.pop(0) for _ in range(n)]
    (ints,) = take(1)
    parts = take(2 * len(plan))
    if depth > 0:
        (head_in,) = take(1)
    take(n_after)
    w_out, small_out, vecs_out, wg_out = take(4)
    if depth == 0:
        (head_out,) = take(1)
    flat, wide, deep, sems = take(4)
    me = ints[2]
    skip = 4 if depth > 0 else 0
    copies = []
    if depth > 0:
        copies.append(pltpu.make_async_copy(head_in, flat.at[0:4], sems.at[len(plan), 0]))
    for t, (axes, start, size) in enumerate(plan):
        for c in range(2):
            for j in range(8):
                away = c + sum(
                    AXIS_VALUE[axis] * ((j >> bit) & 1)
                    for bit, axis in enumerate(axes)
                )
                to = (me ^ away) * tiles + start + skip
                copies.append(
                    pltpu.make_async_copy(
                        parts[2 * t + c].at[j], flat.at[pl.ds(to, size)], sems.at[t, 8 * c + j]
                    )
                )
    for c in copies:
        c.start()
    for c in copies:
        c.wait()
    per = width // LANES
    size = width * per
    base = 4 * size // 8
    for i in range(4):

        def lift(r):
            s = pl.ds(i * size // 8 + r // 8, 12)
            wide[pl.ds(r, 96), :] = flat[s].astype(f32).reshape(96, LANES)

        blocks(size, 96, lift)
        for c in range(per):
            w_out[i, :, c * LANES : (c + 1) * LANES] = wide[
                pl.ds(c, width, stride=per), :
            ].astype(bf16)
    deep[...] = flat[pl.ds(base, deep.shape[0] // 8)].astype(f32).reshape(deep.shape)
    if depth == 0:
        head_out[...] = flat[pl.ds(base + 12, 4)]
    small = jnp.zeros((width, LANES), f32)
    at = 0
    for kinds, first in ((routed, 0), (4, MIX)):
        lines = width * kinds // LANES
        spread = dot(row_picks(width, LANES // kinds), deep[at : at + lines, :].astype(bf16))
        spread = jnp.where(own_lanes(width, kinds), spread, 0.0).astype(bf16)
        small = small + dot(spread, fold_matrix(first, kinds))
        at += lines
    small_out[...] = small.astype(bf16)
    vecs_out[...] = jnp.zeros(vecs_out.shape, f32)
    for r in range(4):
        for c in range(per):
            vecs_out[r : r + 1, c * LANES : (c + 1) * LANES] = deep[at : at + 1, :]
            at += 1
    a = lax.broadcasted_iota(jnp.int32, (LANES, LANES), 0)
    b = lax.broadcasted_iota(jnp.int32, (LANES, LANES), 1)
    if depth > 0:
        line = jnp.broadcast_to(deep[at : at + 1, :], (LANES, LANES))
        line = jnp.where((a == b // routed) & (a < routed), line, 0.0).astype(bf16)
        wg_out[...] = dot(line, fold_matrix(0, routed)).astype(bf16)
    else:
        wg_out[...] = jnp.zeros((LANES, LANES), bf16)


def unpack_layer(ints, parts, plan, head, depth, routed, width, tiles, after=()):
    sds = jax.ShapeDtypeStruct
    per = width // LANES
    outs = [
        sds((4, width, width), bf16),
        sds((width, LANES), bf16),
        sds((8, width), f32),
        sds((LANES, LANES), bf16),
    ]
    args = [ints, *parts]
    if depth > 0:
        args.append(head)
    args += list(after)
    if depth == 0:
        outs.append(sds((4, 8, LANES), bf16))
    got = pl.pallas_call(
        functools.partial(unpack_kernel, (depth, routed, width, tiles, plan, len(after))),
        out_shape=outs,
        in_specs=[SM] + [ANY] * (len(args) - 1),
        out_specs=[VM] * len(outs),
        scratch_shapes=[
            pltpu.VMEM((16 * tiles + 4, 8, LANES), bf16),
            pltpu.VMEM((width * per, LANES), f32),
            pltpu.VMEM((128 if depth == 0 else 104, LANES), f32),
            pltpu.SemaphoreType.DMA((len(plan) + 1, 16)),
        ],
        compiler_params=pltpu.CompilerParams(**PARAMS),
        cost_estimate=pl.CostEstimate(flops=10**9, bytes_accessed=10**7, transcendentals=0),
        name="unpack",
    )(*args)
    return dict(zip(("w", "small", "vecs", "wg"), got[:4])), list(got[4:])


def backward_kernel(static, *refs):
    depth, last, groups, room, packs, tiles, plan, n_after = static
    refs = list(refs)
    take = lambda n: [refs.pop(0) for _ in range(n)]
    (ints, grad_in, w_hbm, small, vecs, wg, cos, sin, side, routes, stream, n1, q_in, k_in, v_in) = take(15)
    mixed, lse, middle = take(3)
    back = take(groups)
    back_g = take(groups)
    if not last:
        (grad_side,) = take(1)
    if depth > 0:
        side_low, routes_low = take(2)
    elif packs:
        (head,) = take(1)
    take(n_after)
    if packs:
        flat_outs = take(2 * len(plan))
    else:
        (flat,) = take(1)
    grad_out, gains = take(2)
    if last:
        (output,) = take(1)
    if depth > 0:
        (grad_carry,) = take(1)
        send = take(groups // 2)
        if packs:
            (head_out,) = take(1)
    if not packs:
        small_out, wg_out = take(2)
    (w, bias, n2h, n2l, table, table_g, hot0, hot1, dn2, gm, gb, dmix, dq, dk, dv, acc, wide, acc_k, acc_v, sems) = take(20)
    if packs:
        flat, flat_sems = take(2)
    count, width = n1.shape
    routed = groups + 4
    per = width // LANES
    size = width * per
    rows = groups * room
    order = (3, 0, 1, 2)
    loads = [pltpu.make_async_copy(w_hbm.at[i], w.at[i], sems.at[i]) for i in range(4)]
    for i in order:
        loads[i].start()
    visible_bias(bias, ints[0], True)
    cols = Columns(side[...], routes[...], groups)
    lane = cols.lane
    g = cols.gates

    add_tables(back, table, room)
    add_tables(back_g, table_g, room)
    at = lax.broadcasted_iota(jnp.int32, (count, rows), 1).astype(f32)
    hot0[...] = jnp.where(at == cols.slots[0], 1.0, 0.0).astype(bf16)
    hot1[...] = jnp.where(at == cols.slots[1], 1.0, 0.0).astype(bf16)
    acc[...] = jnp.zeros(acc.shape, f32)

    def gather(c):
        s = pl.ds(c, LANES)
        grad = grad_in[:, s]
        m = middle[:, s]
        normed = m * cols.inverse_two * vecs[3:4, s]
        high, rest = split(normed)
        n2h[:, s] = high
        n2l[:, s] = rest
        p0 = dot(hot0[...], table[:, s])
        p1 = dot(hot1[...], table[:, s])
        if last:
            y = m + g[0] * p0 + g[1] * p1 + cols.normed_part * normed
            y = y + cols.constant_part[0] * vecs[0:1, s] + cols.constant_part[1] * vecs[1:2, s]
            output[:, s] = y.astype(bf16)
        acc[0] += grad * p0
        acc[1] += grad * p1
        acc[2] += grad * normed
        acc[3] += grad * vecs[0:1, s]
        acc[4] += grad * vecs[1:2, s]
        dn2[:, s] = dot(hot0[...] + hot1[...], table_g[:, s])

    blocks(width, LANES, gather)
    sums = [jnp.sum(acc[i], axis=1, keepdims=True) for i in range(5)]
    on_normed, on_first, on_second = sums[2:]
    by_special = [
        None,
        on_normed,
        cols.first[0] * on_normed + cols.first[1] * on_first,
        cols.second[0] * on_normed + cols.second[1] * on_second,
    ]
    grad_gates = []
    for k in range(2):
        total = sums[k]
        for j in range(1, 4):
            total = total + jnp.where(cols.routes[k] == groups + j, by_special[j], 0.0)
        grad_gates.append(total)
    inner = g[0] * grad_gates[0] + g[1] * grad_gates[1]
    lanes_grad = jnp.zeros((count, LANES), f32)
    for k in range(2):
        lanes_grad = lanes_grad + jnp.where(cols.hot[k], g[k] * (grad_gates[k] - inner), 0.0)
    if not last:
        lanes_grad = lanes_grad + grad_side[...]
    logit_grad = lanes_grad
    for pair, special, constant, first in (
        (cols.first, cols.special[2], on_first, MIX),
        (cols.second, cols.special[3], on_second, MIX + 2),
    ):
        left, right = special * on_normed, special * constant
        middle_sum = pair[0] * left + pair[1] * right
        lanes_grad = lanes_grad + jnp.where(lane == first, pair[0] * (left - middle_sum), 0.0)
        lanes_grad = lanes_grad + jnp.where(lane == first + 1, pair[1] * (right - middle_sum), 0.0)
    high, rest = split(lanes_grad)
    mix_high = jnp.where(lane >= MIX, lanes_grad, 0.0).astype(bf16)
    grad_small = dot_tn(n2h[...], high) + dot_tn(n2h[...], rest) + dot_tn(n2l[...], mix_high)
    if depth > 0:
        lh, lr = split(jnp.where(lane < routed, logit_grad, 0.0))
        grad_carry[...] = jnp.where(lane < routed, dot_nt(lh, wg[...]) + dot_nt(lr, wg[...]), 0.0)
        held = jnp.where(lane < routed, side_low[...], 0.0)
        hh, hr = split(held)
        grad_wg = dot_tn(hh, lh) + dot_tn(hh, lr) + dot_tn(hr, lh)

    def to_middle(c):
        s = pl.ds(c, LANES)
        y = dn2[:, s] + dot_nt(high, small[s, :]) + dot_nt(rest, small[s, :])
        dn2[:, s] = y + grad_in[:, s] * cols.normed_part

    blocks(width, LANES, to_middle)
    acc[0] = jnp.where(lane == 0, cols.constant_part[0], 0.0) + jnp.where(
        lane == 1, cols.constant_part[1], 0.0
    )
    zero = jnp.zeros((8, width), f32)

    def fold(v):
        return jnp.sum(v.reshape(v.shape[0] // 8, 8, width), axis=0)

    def back_norm(i, carry):
        d_gain, d_first, d_second = carry
        s = pl.ds(pl.multiple_of(i * 32, 32), 32)
        ln = lane_of(32)
        inverse = take_lane(side[s, :], ln, INV + 1)
        c0 = take_lane(acc[0, s, :], ln, 0)
        c1 = take_lane(acc[0, s, :], ln, 1)
        x = middle[s, :]
        d = dn2[s, :]
        grad = grad_in[s, :]
        d_gain = d_gain + fold(d * x * inverse)
        d_first = d_first + fold(grad * c0)
        d_second = d_second + fold(grad * c1)
        scaled = d * vecs[3:4, :]
        mean = jnp.mean(x * scaled, axis=1, keepdims=True)
        total = grad + inverse * scaled - x * (inverse * inverse * inverse * mean)
        gm[s, :] = total
        gb[s, :] = total.astype(bf16)
        return d_gain, d_first, d_second

    d_gain, d_first, d_second = lax.fori_loop(0, count // 32, back_norm, (zero, zero, zero))
    line = lambda v: jnp.sum(v, axis=0, keepdims=True)
    gain_two = line(d_gain)
    first_line, second_line = line(d_first), line(d_second)
    loads[3].wait()

    pending = []
    ready = []
    skip = 4 if depth > 0 else 0

    def send_flat(begin, end):
        ready.append((begin, end))
        for shard in range(16):
            low, high = shard * tiles + skip, (shard + 1) * tiles + skip
            covered = sum(max(0, min(high, e) - max(low, b)) for b, e in ready)
            if covered < tiles or shard in pending:
                continue
            pending.append(shard)
            for t in range(len(plan)):
                away_core = (ints[2] ^ shard) & 1
                for c in range(2):

                    @pl.when(away_core == c)
                    def _():
                        flat_copy(shard, t, c).start()

    def flat_copy(shard, t, c):
        away = ints[2] ^ shard
        axes, begin, size = plan[t]
        to = sum(((away // AXIS_VALUE[axis]) & 1) << bit for bit, axis in enumerate(axes))
        source = flat.at[pl.ds(shard * tiles + skip + begin, size)]
        return pltpu.make_async_copy(source, flat_outs[2 * t + c].at[to], flat_sems.at[t, shard])

    def write_flat(i):
        def lower(r):
            s = pl.ds(i * size // 8 + r // 8, 4)
            flat[s] = wide[pl.ds(r, 32), :].reshape(4, 8, LANES).astype(bf16)

        blocks(size, 32, lower)
        if packs:
            send_flat(i * size // 8, (i + 1) * size // 8)

    def weight_grad(i, left, right):
        def piece(c):
            y = dot_tn(left[...], right[:, pl.ds(c, LANES)])
            wide[pl.ds(c // LANES, width, stride=per), :] = y

        blocks(width, LANES, piece)
        write_flat(i)

    weight_grad(3, mixed, gb)

    def to_mixed(c):
        s = pl.ds(c, 256)
        dmix[:, s] = dot_nt(gb[...], w[3, s, :]).astype(bf16)

    blocks(width, 256, to_mixed)
    half_rows = count // 2

    def attend_pair(c):
        t = pl.ds(c, LANES)
        pair = c // LANES
        acc_k[...] = jnp.zeros(acc_k.shape, f32)
        acc_v[...] = jnp.zeros(acc_v.shape, f32)
        for qb in range(2):
            qs = pl.ds(qb * half_rows, half_rows)
            span = (qb + 1) * half_rows
            q2, do2 = q_in[qs, t], dmix[qs, t]
            k2, v2 = k_in[0:span, t], v_in[0:span, t]
            got = None
            for hd in range(2):
                mask = half_mask(hd)
                own = lambda v: v * mask

                km, qm, dom = own(k2), own(q2), own(do2)
                st = dot_nt(km, q2) + bias[0:span, qs]
                pt = jnp.exp(st - lse[pl.ds(2 * pair + hd, 1), qs])
                dpt = dot_nt(v2, dom)
                delta = jnp.sum(pt * dpt, axis=0, keepdims=True)
                dst = (pt * (dpt - delta)).astype(bf16)
                acc_v[0:span, :] += dot(pt.astype(bf16), dom)
                acc_k[0:span, :] += dot(dst, qm)
                y = dot_tn(dst, km)
                got = y if got is None else got + y
            ln = lane_of(half_rows)
            dq[qs, t] = rope_turn(got * 0.125, cos[qs, :], -sin[qs, :], ln).astype(bf16)
        dk[:, t] = rope_turn(acc_k[...], cos[...], -sin[...], lane).astype(bf16)
        dv[:, t] = acc_v[...].astype(bf16)

    blocks(width, LANES, attend_pair)
    for i, right in ((0, dq), (1, dk), (2, dv)):
        loads[i].wait()
    def to_normed(c):
        s = pl.ds(c, 256)
        y = dot_nt(dq[...], w[0, s, :]) + dot_nt(dk[...], w[1, s, :])
        dn2[:, s] = y + dot_nt(dv[...], w[2, s, :])

    blocks(width, 256, to_normed)

    def back_first(i, d_gain):
        s = pl.ds(pl.multiple_of(i * 32, 32), 32)
        inverse = take_lane(side[s, :], lane_of(32), INV)
        x = stream[s, :].astype(f32)
        d = dn2[s, :]
        d_gain = d_gain + fold(d * x * inverse)
        scaled = d * vecs[2:3, :]
        mean = jnp.mean(x * scaled, axis=1, keepdims=True)
        grad_out[s, :] = gm[s, :] + inverse * scaled - x * (inverse * inverse * inverse * mean)
        return d_gain

    gain_one = line(lax.fori_loop(0, count // 32, back_first, zero))
    gains[...] = jnp.zeros(gains.shape, f32)
    gains[0:1, :] = gain_one
    gains[1:2, :] = gain_two
    gains[2:3, :] = first_line
    gains[3:4, :] = second_line
    if depth > 0:
        low_cols = Columns(side_low[...], routes_low[...], groups)
        turned = jnp.transpose(side_low[...])
        at_t = lax.broadcasted_iota(jnp.int32, (rows, count), 0).astype(f32)
        is0 = at_t == turned[SLOT : SLOT + 1, :]
        is1 = at_t == turned[SLOT + 1 : SLOT + 2, :]
        put_grads(low_cols.gates, is0, is1, grad_out, send, room)
    for i, right in ((0, dq), (1, dk), (2, dv)):
        weight_grad(i, n1, right)
    if not packs:
        small_out[...] = grad_small.astype(bf16).astype(f32)
        low_wg = grad_wg.astype(bf16) if depth > 0 else jnp.zeros(wg_out.shape, bf16)
        wg_out[...] = low_wg.astype(f32)
        return
    tail = wide
    start = 0
    small_low = grad_small.astype(bf16)
    for kinds, first in ((routed, 0), (4, MIX)):
        lines = width * kinds // LANES
        spread = dot_nt(small_low, fold_matrix(first, kinds))
        spread = jnp.where(own_lanes(width, kinds), spread, 0.0).astype(bf16)
        tail[start : start + lines, :] = dot_tn(row_picks(width, LANES // kinds), spread)
        start += lines
    for row in (first_line, second_line, gain_one, gain_two):
        for c in range(per):
            tail[start : start + 1, :] = row[:, c * LANES : (c + 1) * LANES]
            start += 1
    used = 4 * size // 8 + start // 8
    flat[pl.ds(4 * size // 8, start // 8)] = (
        tail[0:start, :].reshape(start // 8, 8, LANES).astype(bf16)
    )
    a = lax.broadcasted_iota(jnp.int32, (8, LANES), 0)
    if depth > 0:
        ra = lax.broadcasted_iota(jnp.int32, (LANES, LANES), 0)
        rb = lax.broadcasted_iota(jnp.int32, (LANES, LANES), 1)
        spread = dot_nt(grad_wg.astype(bf16), fold_matrix(0, routed))
        spread = jnp.where((ra == rb // routed) & (ra < routed), spread, 0.0)
        one = jnp.sum(spread, axis=0, keepdims=True)
        flat[pl.ds(used, 1)] = jnp.where(a == 0, one, 0.0).reshape(1, 8, LANES).astype(bf16)
        left = flat.shape[0] - used - 1
        if left > 0:
            flat[pl.ds(used + 1, left)] = jnp.zeros((left, 8, LANES), bf16)
        head_out[...] = flat[0:4]
    else:
        flat[pl.ds(used, 4)] = head[...]
    send_flat(4 * size // 8, flat.shape[0])
    for t in range(len(plan)):
        for shard in range(16):
            flat_copy(shard, t, shard % 2).wait()


def layer_backward(
    depth, sizes, ints, grad_in, weights, tables, held, tabs, extra, packs, tiles, plan, after=()
):
    groups, room = sizes
    last = depth == LAYERS - 1
    count, width = held["n1"].shape
    rows = groups * room
    per = width // LANES
    sds = jax.ShapeDtypeStruct
    args = [
        ints, grad_in, weights["w"], weights["small"], weights["vecs"], weights["wg"], *tables,
        held["side"], held["routes"], held["stream"], held["n1"], held["q"], held["k"], held["v"],
        held["mixed"], held["lse"], held["middle"], *tabs, *extra,
    ]
    specs = [SM, VM, ANY] + [VM] * (len(args) - 3) + [ANY] * len(after)
    args += list(after)
    if packs:
        outs = [sds((8, size, 8, LANES), bf16) for _, _, size in plan for c in range(2)]
    else:
        outs = [sds((4 * width * per // 8, 8, LANES), bf16)]
    out_specs = [ANY if packs else VM] * len(outs)
    outs += [sds((count, width), f32), sds((8, width), f32)]
    if last:
        outs.append(sds((count, width), bf16))
    if depth > 0:
        outs += [sds((count, LANES), f32)] + [sds((2 * room, width), bf16)] * (groups // 2)
        if packs:
            outs.append(sds((4, 8, LANES), bf16))
    if not packs:
        outs += [sds((width, LANES), f32), sds((LANES, LANES), f32)]
    out_specs += [VM] * (len(outs) - len(out_specs))
    low = pltpu.VMEM((count, width), bf16)
    full = pltpu.VMEM((count, width), f32)
    side = pltpu.VMEM((count, LANES), f32)
    hot = pltpu.VMEM((count, rows), bf16)
    tab = pltpu.VMEM((rows, width), bf16)
    scratch = [
        pltpu.VMEM((4, width, width), bf16), pltpu.VMEM((count, count), f32), low, low, tab, tab, hot, hot,
        full, full, low, low, low, low, low, pltpu.VMEM((5, count, LANES), f32),
        pltpu.VMEM((width * per, LANES), f32), side, side, pltpu.SemaphoreType.DMA((4,)),
    ]
    if packs:
        scratch.append(pltpu.VMEM((16 * tiles + (4 if depth > 0 else 0), 8, LANES), bf16))
        scratch.append(pltpu.SemaphoreType.DMA((len(plan), 16)))
    got = pl.pallas_call(
        functools.partial(backward_kernel, (depth, last, groups, room, packs, tiles, plan, len(after))),
        out_shape=outs,
        in_specs=specs,
        out_specs=out_specs,
        scratch_shapes=scratch,
        compiler_params=pltpu.CompilerParams(**PARAMS),
        cost_estimate=pl.CostEstimate(
            flops=14 * 10**9, bytes_accessed=30 * 10**6, transcendentals=4 * 10**6
        ),
        name="layer_backward",
    )(*args)
    return list(got)


def rope_tables(count):
    lane = np.arange(LANES)
    frequency = rope_base ** (-(lane % 32).astype(np.float32) / np.float32(32))
    angle = np.arange(count, dtype=np.float32)[:, None] * frequency[None, :].astype(np.float32)
    sign = np.where(lane % 64 < 32, -1.0, 1.0)
    cos, sin = np.cos(angle), np.sin(angle) * sign[None, :]
    return jnp.asarray(cos.astype(np.float32)), jnp.asarray(sin.astype(np.float32))


def unpack_plain(flat, routed, width):
    params = [dict() for depth in range(LAYERS)]
    params = unpack(flat, width, routed)
    out = []
    for p in params:
        small = jnp.zeros((width, LANES), bf16)
        small = small.at[:, :routed].set(p["router"]).at[:, MIX : MIX + 4].set(p["mixing"])
        vecs = jnp.zeros((8, width), f32)
        vecs = vecs.at[0:2].set(p["constant"].astype(f32))
        vecs = vecs.at[2].set(p["attn_gain"].astype(f32)).at[3].set(p["moe_gain"].astype(f32))
        wg = jnp.zeros((LANES, LANES), bf16)
        if "carry" in p:
            wg = wg.at[:routed, :routed].set(p["carry"])
        w = jnp.stack([p[n] for n in ("query", "key", "value", "output")])
        out.append(dict(w=w, small=small, vecs=vecs, wg=wg))
    return out


def on_device(
    tokens_in,
    cotangent,
    seq_lengths,
    drop_order,
    routes,
    dense_master,
    dense_moment,
    dense_second,
    expert_master,
    expert_moment,
    expert_second,
):
    count, width = tokens_in.shape
    wires = Wires()
    groups = wires.groups
    routed = groups + 4
    capacity = max(2, 45 * count // (32 * routed))
    room = -(-capacity // 16) * 16
    sizes = (groups, capacity, room)
    whole_size = dense_master.shape[0] * wires.dp * groups
    order = drop_order[0]
    place = (wires.me_dp % 4) * 4 + wires.me_group
    ints = jnp.stack([seq_lengths[0], wires.me_group.astype(jnp.int32), place.astype(jnp.int32)])
    tables = rope_tables(count)
    tiles = dense_master.shape[0] // (8 * LANES)
    packs = (
        LANES % routed == 0
        and (wires.tops, groups) == (2, 4)
        and dense_master.shape[0] == tiles * 8 * LANES
    )
    bsizes = (groups, room)
    half = groups // 2
    thirds, halves = plan_thirds(tiles), plan_halves(tiles)

    dense_low = dense_master.astype(bf16)
    expert_low = [expert_master[0, depth].astype(bf16) for depth in range(LAYERS)]
    far = range(1, wires.tops)
    if packs:
        shard = dense_low.reshape(tiles, 8, LANES)
        top = wires.me_dp >= 4
        other = wires.swap(shard, h=1)
        pieces = [jnp.where(top, other, shard), jnp.where(top, shard, other)]
        dense0 = [pieces[0][None, a : a + n] for _, a, n in thirds]
        for step in range(3):
            dense0 = grow(wires, dense0, thirds, step)
            if step == 0:
                whole = pin(pieces[1][None], dense0)
                dense1 = jnp.concatenate([whole, wires.swap(whole, l=1)], axis=0)
        go = tuple(dense0)
        cores = [wires.swap(v, g=1) for v in dense0]
        parts = [v for pair in zip(dense0, cores) for v in pair]
        dense1 = [pin(dense1, *go)[:, a : a + n] for _, a, n in halves]
        dense1 = grow(wires, dense1, halves, 1)
        first, (head,) = unpack_layer(ints, parts, thirds, None, 0, routed, width, tiles)
    else:
        full = lax.all_gather(dense_low, ALL, axis=0, tiled=True)
        first, second = unpack_plain(full, routed, width)
        go = (first["vecs"],)
    expert_low[0] = pin(expert_low[0], *go)
    got_far = [wires.swap(v, h=h) for h in far for v in cut_far(expert_low[0])]
    near = wires.swap(expert_low[0], x=1)

    names = ("n1", "q", "k", "v", "mixed", "lse", "middle", "side", "stream")
    got = layer_forward(0, sizes, ints, order, routes[0], first, [tokens_in], tables)
    held0 = dict(zip(names, got[half:]), stream=tokens_in, routes=routes[0])
    gone = held0["side"]
    cross_far = [wires.swap(pin(v, gone), x=1) for v in got_far[:-1]]
    if packs:
        dense1 = grow(wires, [pin(v, gone) for v in dense1], halves, 2)
    arrived0 = exchange_out(wires, got[:half])
    cross_far.append(wires.swap(pin(got_far[-1], arrived0[1]), x=1))
    expert0 = [expert_low[0], near]
    for pair in zip(got_far, cross_far):
        expert0 += list(pair)
    low1 = pin(cut_far(expert_low[1]), *arrived0)
    got_far1 = [wires.swap(low1[0], h=h) for h in far]
    near0, crossed0, _ = run_expert(expert0, arrived0, None, room)
    near1 = wires.swap(pin(expert_low[1], near0), x=1)
    ret0 = exchange_back(wires, near0, crossed0)
    if packs:
        dense1 = pin(dense1, near0)
        cores = [wires.swap(v, g=1) for v in dense1]
        parts = [v for pair in zip(dense1, cores) for v in pair]
        second, _ = unpack_layer(ints, parts, halves, head, 1, routed, width, tiles)
    weights = [first, second]
    low1 = pin(low1, *ret0)
    last_far1 = [wires.swap(low1[1], h=h) for h in far]
    cross_far1 = [wires.swap(pin(v, *ret0), x=1) for v in got_far1]

    source = [
        held0["side"], routes[0], held0["middle"], weights[0]["vecs"], weights[1]["wg"], cotangent, *ret0,
    ]
    got = layer_forward(1, sizes, ints, order, routes[1], second, source, tables)
    held1 = dict(zip(names, got[groups:]), routes=routes[1])
    arrived1 = exchange_out(wires, got[:half])
    last_cross1 = [wires.swap(pin(v, held1["side"]), x=1) for v in last_far1]
    expert1 = [expert_low[1], near1]
    for four in zip(got_far1, cross_far1, last_far1, last_cross1):
        expert1 += list(four)
    grads1 = exchange_out(wires, pin(got[half:groups], *arrived1))
    out1, crossed1, _ = run_expert(expert1, arrived1, None, room)
    ret1 = exchange_back(wires, out1, pin(crossed1, *grads1))
    out1, crossed1, parts1 = run_expert(expert1, arrived1, grads1, room)
    sum1 = ScatterExpert(wires, parts1)
    sum1.first()
    back1 = exchange_back(wires, out1, crossed1)
    sum1.second(*back1)

    got = layer_backward(
        1, bsizes, ints, cotangent, second, tables, held1, [*ret1, *back1],
        [held0["side"], routes[0]], packs, tiles, halves,
    )
    n_flat = 2 * len(halves) if packs else 1
    flat1, got = got[:n_flat], got[n_flat:]
    grad1, gains1, output, grad_side = got[:4]
    rest1 = got[4 + half :]
    if packs:
        dense1 = ScatterDense(wires, list(zip(flat1[0::2], flat1[1::2])), halves)
        dense1.send(0)
    grads0 = exchange_out(wires, pin(got[4 : 4 + half], *sum1.received()))
    if packs:
        dense1.add()
        dense1.send(1, *grads0)
    out0, crossed0, parts0 = run_expert(expert0, arrived0, grads0, room)
    sum0 = ScatterExpert(wires, parts0)
    sum0.first()
    back0 = exchange_back(wires, out0, crossed0)
    if packs:
        dense1.add()
        dense1.send(2, out0)
        dense1.add()
    sum0.second(*back0)
    extra = [grad_side]
    if packs:
        dense1.send(3, *back0)
        dense1.add()
        extra.append(rest1[0])

    got = layer_backward(
        0, bsizes, ints, grad1, first, tables, held0, [*ret0, *back0], extra,
        packs, tiles, thirds,
    )
    n_flat = 2 * len(thirds) if packs else 1
    flat0, got = got[:n_flat], got[n_flat:]
    grad_stream, gains0 = got[:2]
    flat0, *_ = pin(flat0, *sum0.received()), None
    shard1 = sum1.done()
    shard0 = sum0.done()
    if packs:
        dense0 = ScatterDense(wires, list(zip(flat0[0::2], flat0[1::2])), thirds)
        for step in range(4):
            dense0.send(step)
            dense0.add()
        both = [dense0.done(), dense1.done()]
        give = jnp.where(top, both[0], both[1])
        keep = jnp.where(top, both[1], both[0])
        dense_shard = keep.astype(f32) + wires.swap(give, h=1).astype(f32)
    else:
        pieces = []
        for flat, gains, (small, wg) in ((flat0[0], gains0, got[2:4]), (flat1[0], gains1, rest1)):
            pieces += [flat.reshape(-1), small[:, :routed].reshape(-1)]
            pieces += [small[:, MIX : MIX + 4].reshape(-1)]
            pieces += [gains[2:4].reshape(-1), gains[0:2].reshape(-1)]
        pieces.append(wg[:routed, :routed].reshape(-1))
        flat = jnp.concatenate([p.astype(bf16) for p in pieces])
        flat = jnp.concatenate([flat, jnp.zeros((whole_size - flat.shape[0],), bf16)])
        dense_shard = lax.psum_scatter(flat, ALL, scatter_dimension=0, tiled=True)
    dense_shard = dense_shard.astype(f32).reshape(-1)
    expert_shard = jnp.stack([shard0, shard1], axis=0)[None]
    gain_local = jnp.stack([gains0[0:2], gains1[0:2]], axis=0)
    local_square = jnp.sum(dense_shard * dense_shard) + jnp.sum(expert_shard * expert_shard)
    if packs:
        payload = jnp.concatenate([gain_local.reshape(4, width), jnp.zeros((4, width), f32)], axis=0)
        payload = payload.at[4].set(local_square)
        for step in (dict(g=1), dict(x=1), dict(g=2), dict(l=1), dict(h=1)):
            payload = payload + wires.swap(payload, **step)
        gain_total = payload[:4].reshape(2, 2, width)
        square_sum = payload[4, 0]
    else:
        square_sum, gain_total = lax.psum((local_square, gain_local), ALL)
    factor = jnp.minimum(1.0, clip_norm / (jnp.sqrt(square_sum) + 1e-06))
    dense_clip = dense_shard * factor
    expert_clip = expert_shard * factor
    dense_step = adam_delta(dense_master, dense_moment, dense_second, dense_clip)
    expert_step = adam_delta(expert_master, expert_moment, expert_second, expert_clip)
    return (
        output,
        grad_stream,
        dense_clip,
        expert_clip,
        gain_total * factor,
        dense_step,
        expert_step,
    )


def solution(mesh):
    return jax.shard_map(
        on_device,
        mesh=mesh,
        in_specs=(
            P(("dp", "group"), None),
            P(("dp", "group"), None),
            P(("dp", "group")),
            P(("dp", "group"), None),
            P(None, ("dp", "group"), None),
            P(("dp", "group")),
            P(("dp", "group")),
            P(("dp", "group")),
            P("group", None, None, "dp", None),
            P("group", None, None, "dp", None),
            P("group", None, None, "dp", None),
        ),
        out_specs=(
            P(("dp", "group"), None),
            P(("dp", "group"), None),
            P(("dp", "group")),
            P("group", None, None, "dp", None),
            P(),
            P(("dp", "group")),
            P("group", None, None, "dp", None),
        ),
        check_vma=False,
    )
```
